256 devices in a mesh: pipe: 2 (over x_lo), ctx: 16 (over x_hi, z), tp: 8 (over y, core).
Axes of the slice: x: 4 (x_hi: 2, x_lo: 2; x = x_hi * 2 + x_lo), y: 4, z: 8, core: 2. Of those that a mesh axis runs over, the one named last changes fastest.
Arguments:
- fwd_queries: bfloat16 [2, 2048, 8192], P('pipe', 'ctx', 'tp'), may hold values from -6 to 6
- fwd_keyvals: bfloat16 [2, 2, 2048, 1024], P('pipe', None, 'ctx', 'tp'), may hold values from -6 to 6
- bwd_queries: bfloat16 [2, 2048, 8192], P('pipe', 'ctx', 'tp'), may hold values from -6 to 6
- bwd_keyvals: bfloat16 [2, 2, 2048, 1024], P('pipe', None, 'ctx', 'tp'), may hold values from -6 to 6
- bwd_cotangent: bfloat16 [2, 2048, 8192], P('pipe', 'ctx', 'tp'), may hold values from -6 to 6
- doc_lengths: int32 [2, 8], replicated, may hold values from 1 to 1024, 2048 in all within a row
- block_order: int32 [2, 16], replicated, may hold values from 0 to 15, each once within a row
Outputs:
- arrived_output: bfloat16 [2, 2048, 8192], P('pipe', 'ctx', 'tp')
- arrived_query_grad: bfloat16 [2, 2048, 8192], P('pipe', 'ctx', 'tp')
- arrived_keyval_grad: bfloat16 [2, 2, 2048, 1024], P('pipe', None, 'ctx', 'tp')
The draws below stay inside these ranges and needn't reach their ends.
Inputs may be any that keep to these rules, and one draw needn't show every extreme that they name: `block_order`: each row is a permutation of 0 to 15. `doc_lengths`: each row sums to 2048.
All inputs are finite; a program needn't handle non-finite values.
Results may differ from the reference program's by a relative error of at most 0.023.
Values may be sent and summed in bfloat16 or wider, within the bound.
No kernel may reach another device: no remote copies, remote signals or barrier semaphores. Data moves between devices by JAX's collectives and lax.ppermute only.
A program may use at most 64 MiB of HBM per device.

```python
import math
import jax
import jax.numpy as jnp
import numpy as np
from jax import lax

HEADS = 64
KVH = 8
HD = 128
BLOCK = 128
NDOC = 8
SEQ = 2048
NBLK = 16


def plant_layout(key, salt):
    key = jax.random.fold_in(key, salt)
    sign_key, pick_key = jax.random.split(key)
    signs = jnp.where(jax.random.bernoulli(sign_key, 0.5, (2, HD)), 1.0, -1.0).astype(jnp.float32)
    offsets = jax.random.randint(pick_key, (2, NBLK), 1, BLOCK)
    index = jnp.arange(SEQ, dtype=jnp.int32)
    picked = jnp.repeat(offsets, BLOCK, axis=1, total_repeat_length=SEQ)
    chosen = (index % BLOCK)[None, :] == picked
    levels = jnp.array([4.5, 5.0, 5.5, 6.0], jnp.float32)
    strength = levels[index // BLOCK % 4]
    return (signs, chosen, strength)


def plant_queries(field, signs, chosen, strength):
    pattern = jnp.tile(signs, (1, HEADS))
    planted = strength[None, :, None] * pattern[:, None, :]
    return jnp.where(chosen[:, :, None], planted, field)


def plant_keys(field, signs, chosen, strength):
    pattern = jnp.tile(signs, (1, KVH))
    damping = jnp.tile(jnp.where(jnp.arange(HD) < 2, 0.6, 1.0).astype(jnp.float32), KVH)
    planted = strength[None, :, None] * pattern[:, None, :]
    earlier = jnp.roll(chosen, -1, axis=1)
    keys = jnp.where(chosen[:, :, None], planted, jnp.where(earlier[:, :, None], planted * damping[None, None, :], field[:, 0]))
    return jnp.stack([keys, field[:, 1]], axis=1)


def draw_fwd_queries(key, part):
    signs, chosen, strength = plant_layout(key, 101)
    key = jax.random.fold_in(key, 1)
    shape = (2, SEQ, HEADS * HD)
    field = jnp.clip(jax.random.normal(key, shape, jnp.float32), -6.0, 6.0)
    return plant_queries(field, signs, chosen, strength).astype(jnp.bfloat16)


def draw_fwd_keyvals(key, part):
    signs, chosen, strength = plant_layout(key, 101)
    key = jax.random.fold_in(key, 2)
    shape = (2, 2, SEQ, KVH * HD)
    field = jnp.clip(jax.random.normal(key, shape, jnp.float32), -6.0, 6.0)
    return plant_keys(field, signs, chosen, strength).astype(jnp.bfloat16)


def draw_bwd_queries(key, part):
    signs, chosen, strength = plant_layout(key, 202)
    key = jax.random.fold_in(key, 3)
    shape = (2, SEQ, HEADS * HD)
    field = jnp.clip(jax.random.normal(key, shape, jnp.float32), -6.0, 6.0)
    return plant_queries(field, signs, chosen, strength).astype(jnp.bfloat16)


def draw_bwd_keyvals(key, part):
    signs, chosen, strength = plant_layout(key, 202)
    key = jax.random.fold_in(key, 4)
    shape = (2, 2, SEQ, KVH * HD)
    field = jnp.clip(jax.random.normal(key, shape, jnp.float32), -6.0, 6.0)
    return plant_keys(field, signs, chosen, strength).astype(jnp.bfloat16)


def steps_of(key, extent, pieces, least, top_value):
    gain, own = 1.0, jax.random.fold_in(key, 6)
    for axis_at, parts in pieces:
        steps = jnp.exp(jax.random.uniform(jax.random.fold_in(own, axis_at), (parts,), jnp.float32, least / len(pieces), top_value / len(pieces)))
        gain = gain * jnp.repeat(steps, extent[axis_at] // parts).reshape([-1 if axis == axis_at else 1 for axis in range(len(extent))])
    return gain


def profile(number_of, total, most, slope):
    portions = [(1 << 20) // math.isqrt(rank ** slope) + 1 for rank in range(2, number_of + 1)]
    rest, holding = total - most - (number_of - 1), [1] * (number_of - 1)
    while rest > 0:
        movable = [i for i in range(number_of - 1) if holding[i] < most]
        whole, remaining = sum([portions[i] for i in movable]), rest
        for i in movable:
            extra = min(most - holding[i], max(1, remaining * portions[i] // whole), rest)
            holding[i] = holding[i] + extra
            rest = rest - extra
    return np.array([most] + holding)


def ragged_sizes(own_key, count, total, bound, lean):
    if count == 2:
        one = jax.random.randint(own_key, (), max(1, total - bound), min(bound, total - 1) + 1)
        return jnp.stack([one, total - one])
    sizes = jnp.asarray(profile(count, total, bound, lean), jnp.int32)
    twos = (count - 1) // 2
    source_of, sink = sizes[1:1 + 2 * twos:2], sizes[2:2 + 2 * twos:2]
    margin = jnp.minimum(source_of - 1, bound - sink)
    moved = jax.random.randint(jax.random.fold_in(own_key, 1), (twos,), 0, 1 << 20) % (margin + 1)
    sizes = sizes.at[1:1 + 2 * twos:2].set(source_of - moved).at[2:2 + 2 * twos:2].set(sink + moved)
    return sizes[jax.random.permutation(jax.random.fold_in(own_key, 2), count)]


def centred(rng, extent, scale, most, cuts=(), kind=jnp.bfloat16):
    values = scale * jax.random.normal(rng, extent, jnp.float32)
    if cuts:
        values = values * steps_of(rng, extent, cuts, -0.22, 0.18)
    return jnp.clip(values, -most, most).astype(kind)


def setup_inputs(seed: int = 0) -> dict:
    arg_keys = jax.random.split(jax.random.key(seed), 8)
    fwd_queries = draw_fwd_queries(jax.random.fold_in(arg_keys[7], 71), 0)
    fwd_keyvals = draw_fwd_keyvals(jax.random.fold_in(arg_keys[7], 71), 0)
    bwd_queries = draw_bwd_queries(jax.random.fold_in(arg_keys[7], 71), 0)
    bwd_keyvals = draw_bwd_keyvals(jax.random.fold_in(arg_keys[7], 71), 0)
    bwd_cotangent = centred(arg_keys[4], (2, SEQ, HEADS * HD), 1.0, 6.0, ((0, 2), (1, 16), (2, 8)))
    doc_lengths = jax.vmap(lambda own: ragged_sizes(own, NDOC, SEQ, SEQ // 2, 2))(jax.random.split(arg_keys[5], 2)).reshape((2, NDOC)).astype(jnp.int32)
    block_order = jax.vmap(lambda own: jax.random.permutation(own, NBLK))(jax.random.split(arg_keys[6], 2)).reshape((2, NBLK)).astype(jnp.int32)
    return dict(fwd_queries=fwd_queries, fwd_keyvals=fwd_keyvals, bwd_queries=bwd_queries, bwd_keyvals=bwd_keyvals, bwd_cotangent=bwd_cotangent, doc_lengths=doc_lengths, block_order=block_order)


def token_layout(order, lengths):
    index = jnp.arange(SEQ, dtype=jnp.int32)
    position = order[index // BLOCK] * BLOCK + index % BLOCK
    ends = jnp.cumsum(lengths)
    document = jnp.sum((position[:, None] >= ends[None, :]).astype(jnp.int32), axis=1)
    return position, document


def allowed_pairs(order, lengths):
    position, document = token_layout(order, lengths)
    same = document[:, None] == document[None, :]
    causal = position[None, :] <= position[:, None]
    return same & causal


def to_groups(queries):
    group = HEADS // KVH
    return queries.reshape(SEQ, KVH, group, HD).transpose(1, 0, 2, 3)


def to_keys(keyvals):
    return keyvals.reshape(SEQ, KVH, HD).transpose(1, 0, 2)


def softmax_stats(query, key, value, mask):
    scale = HD ** -0.5
    scores = jnp.einsum('qgd,kd->gqk', query.astype(jnp.float32), key.astype(jnp.float32)) * scale
    scores = jnp.where(mask[None], scores, -1e30)
    top = jnp.max(scores, axis=-1)
    probs = jnp.where(mask[None], jnp.exp(scores - top[..., None]), 0.0)
    total = jnp.sum(probs, axis=-1)
    rounded = lax.optimization_barrier(probs.astype(jnp.bfloat16)).astype(jnp.float32)
    acc = jnp.einsum('gqk,kd->gqd', rounded, value.astype(jnp.float32))
    return scores, top, total, acc


def forward_group(items, mask):
    query, key, value = items
    scores, top, total, acc = softmax_stats(query, key, value, mask)
    return (acc / total[..., None]).astype(jnp.bfloat16).transpose(1, 0, 2)


def backward_group(items, mask):
    query, key, value, cotan = items
    scale = HD ** -0.5
    scores, top, total, acc = softmax_stats(query, key, value, mask)
    outcome = acc / total[..., None]
    lse = top + jnp.log(total)
    probs = jnp.where(mask[None], jnp.exp(scores - lse[..., None]), 0.0)
    rounded = lax.optimization_barrier(probs.astype(jnp.bfloat16)).astype(jnp.float32)
    cot = cotan.astype(jnp.float32)
    value_grad = jnp.einsum('gqk,qgd->kd', rounded, cot)
    dprobs = jnp.einsum('qgd,kd->gqk', cot, value.astype(jnp.float32))
    delta = jnp.einsum('qgd,gqd->gq', cot, outcome)
    dscores = probs * (dprobs - delta[..., None])
    drounded = lax.optimization_barrier(dscores.astype(jnp.bfloat16)).astype(jnp.float32)
    query_grad = jnp.einsum('gqk,kd->qgd', drounded, key.astype(jnp.float32)) * scale
    key_grad = jnp.einsum('gqk,qgd->kd', drounded, query.astype(jnp.float32)) * scale
    return query_grad.astype(jnp.bfloat16), key_grad.astype(jnp.bfloat16), value_grad.astype(jnp.bfloat16)


def reference(fwd_queries, fwd_keyvals, bwd_queries, bwd_keyvals, bwd_cotangent, doc_lengths, block_order):
    forward_mask = allowed_pairs(block_order[1], doc_lengths[1])
    backward_mask = allowed_pairs(block_order[0], doc_lengths[0])
    outputs = []
    query_grads = []
    keyval_grads = []
    for section in range(2):
        query = to_groups(fwd_queries[section])
        key = to_keys(fwd_keyvals[section, 0])
        value = to_keys(fwd_keyvals[section, 1])
        result = lax.map(lambda items: forward_group(items, forward_mask), (query, key, value))
        outputs.append(result.transpose(1, 0, 2, 3).reshape(SEQ, HEADS * HD))
        query = to_groups(bwd_queries[section])
        key = to_keys(bwd_keyvals[section, 0])
        value = to_keys(bwd_keyvals[section, 1])
        cotan = to_groups(bwd_cotangent[section])
        dquery, dkey, dvalue = lax.map(lambda items: backward_group(items, backward_mask), (query, key, value, cotan))
        query_grads.append(dquery.transpose(1, 0, 2, 3).reshape(SEQ, HEADS * HD))
        dkey = dkey.transpose(1, 0, 2).reshape(SEQ, KVH * HD)
        dvalue = dvalue.transpose(1, 0, 2).reshape(SEQ, KVH * HD)
        keyval_grads.append(jnp.stack([dkey, dvalue]))
    arrived_output = jnp.stack([outputs[1], outputs[0]])
    arrived_query_grad = jnp.stack([query_grads[1], query_grads[0]])
    arrived_keyval_grad = jnp.stack([keyval_grads[1], keyval_grads[0]])
    return arrived_output, arrived_query_grad, arrived_keyval_grad
```

```python
import jax
import jax.numpy as jnp
from jax import lax
from jax.experimental import pallas as pl
from jax.experimental.pallas import tpu as pltpu
from jax.sharding import PartitionSpec as P

HD = 128
BLOCK = 128
GROUP = 8
ROWS = GROUP * BLOCK
WIDE = 2 * BLOCK
SLOTS = 16
RING = 8
OFFSETS = (0, -3, 3, -1, -4, 2, 1, -2)
SCALE = HD**-0.5
LOG2E = 1.4426950408889634
NEG = -1e30


def prepare(batch, order, lens, slots, bases):
    me = lax.axis_index("ctx")
    half, z = me // RING, me % RING
    query_base = order[batch, me] * BLOCK
    place = query_base + lax.broadcasted_iota(jnp.int32, (1, BLOCK), 1)
    first = jnp.zeros((1, BLOCK), jnp.int32)
    least = jnp.int32(0)
    end = jnp.int32(0)
    for i in range(lens.shape[1]):
        end = end + lens[batch, i]
        first = jnp.where(place >= end, end, first)
        least = jnp.where(query_base >= end, end, least)
    count = jnp.int32(0)
    for slot in range(SLOTS):
        side = half if slot < RING else 1 - half
        owner = side * RING + (z + (OFFSETS[slot % RING] + RING)) % RING
        base = order[batch, owner] * BLOCK
        slots[count] = slot
        bases[count] = base
        active = (base <= query_base) & (base + (BLOCK - 1) >= least)
        count = count + active.astype(jnp.int32)
    return count, first, place


def dot(a, b):
    return jnp.dot(a, b, preferred_element_type=jnp.float32)


def columns(ref, dst, rows_dst=None):
    for h in range(GROUP):
        part = ref[0, :, h * HD : (h + 1) * HD]
        dst[:, h * BLOCK : (h + 1) * BLOCK] = part.T
        if rows_dst is not None:
            rows_dst[h * BLOCK : (h + 1) * BLOCK, :] = part


def softmax_passes(count, first, place, slots, bases, kv, q_t, probs, acc):
    def scores(i, top):
        slot, base = slots[i], bases[i]
        key = kv[slot, 0]
        row = base + lax.broadcasted_iota(jnp.int32, (BLOCK, BLOCK), 0)
        mask = (row >= first) & (row <= place)
        tops = []
        for c in range(ROWS // WIDE):
            s = dot(key, q_t[:, c * WIDE : (c + 1) * WIDE])
            for j in range(WIDE // BLOCK):
                part = jnp.where(mask, s[:, j * BLOCK : (j + 1) * BLOCK], NEG)
                at = c * WIDE + j * BLOCK
                probs[i, :, at : at + BLOCK] = part
                tops.append(jnp.max(part.reshape(BLOCK // 8, 8, BLOCK), axis=0))
        return jnp.maximum(top, jnp.concatenate(tops, axis=1))

    top = lax.fori_loop(0, count, scores, jnp.full((8, ROWS), NEG, jnp.float32))
    top = jnp.max(top, axis=0, keepdims=True)
    acc[...] = jnp.zeros_like(acc)

    def sums(i, total):
        value_t = kv[slots[i], 1].T
        totals = []
        for c in range(ROWS // WIDE):
            at = slice(c * WIDE, (c + 1) * WIDE)
            p = jnp.exp2((probs[i, :, at] - top[:, at]) * (SCALE * LOG2E))
            probs[i, :, at] = p
            totals.append(jnp.sum(p.reshape(BLOCK // 8, 8, WIDE), axis=0))
            acc[:, at] += dot(value_t, p.astype(jnp.bfloat16))
        return total + jnp.concatenate(totals, axis=1)

    total = lax.fori_loop(0, count, sums, jnp.zeros((8, ROWS), jnp.float32))
    return jnp.sum(total, axis=0, keepdims=True)


def forward_kernel(order, lens, q, near, far, out, slots, bases, kv, q_t, probs, acc):
    count, first, place = prepare(1, order, lens, slots, bases)
    columns(q, q_t)
    kv[:RING] = near[...]
    kv[RING:] = far[...]
    total = softmax_passes(count, first, place, slots, bases, kv, q_t, probs, acc)
    inverse = 1.0 / total
    for h in range(GROUP):
        at = slice(h * BLOCK, (h + 1) * BLOCK)
        out[0, :, at] = (acc[:, at] * inverse[:, at]).T.astype(jnp.bfloat16)


def backward_kernel(
    order, lens, q, cotan, near, far, dq, dnear, dfar,
    slots, bases, kv, q_t, c_t, q_rows, c_rows, probs, acc, dkv,
):
    count, first, place = prepare(0, order, lens, slots, bases)
    columns(q, q_t, q_rows)
    columns(cotan, c_t, c_rows)
    kv[:RING] = near[...]
    kv[RING:] = far[...]
    total = softmax_passes(count, first, place, slots, bases, kv, q_t, probs, acc)
    inverse = 1.0 / total
    delta = jnp.sum(c_t[...].astype(jnp.float32) * acc[...], axis=0, keepdims=True) * inverse
    acc[...] = jnp.zeros_like(acc)
    dkv[...] = jnp.zeros_like(dkv)

    def grads(i, _):
        slot = slots[i]
        key_t = kv[slot, 0].T
        value = kv[slot, 1]
        dk = jnp.zeros((BLOCK, HD), jnp.float32)
        dv = jnp.zeros((BLOCK, HD), jnp.float32)
        for c in range(ROWS // WIDE):
            at = slice(c * WIDE, (c + 1) * WIDE)
            p = probs[i, :, at] * inverse[:, at]
            dp = dot(value, c_t[:, at])
            ds = (p * (dp - delta[:, at])).astype(jnp.bfloat16)
            dv += dot(p.astype(jnp.bfloat16), c_rows[at, :])
            dk += dot(ds, q_rows[at, :])
            acc[:, at] += dot(key_t, ds)
        dkv[slot, 0] = (dk * SCALE).astype(jnp.bfloat16)
        dkv[slot, 1] = dv.astype(jnp.bfloat16)
        return 0

    lax.fori_loop(0, count, grads, 0)
    for h in range(GROUP):
        at = slice(h * BLOCK, (h + 1) * BLOCK)
        dq[0, :, at] = (acc[:, at] * SCALE).T.astype(jnp.bfloat16)
    dnear[...] = dkv[:RING]
    dfar[...] = dkv[RING:]


SMEM = pl.BlockSpec(memory_space=pltpu.SMEM)
VMEM = pl.BlockSpec(memory_space=pltpu.VMEM)
HALF = jax.ShapeDtypeStruct((RING, 2, BLOCK, HD), jnp.bfloat16)
WHOLE = jax.ShapeDtypeStruct((1, BLOCK, GROUP * HD), jnp.bfloat16)
LIST = pltpu.SMEM((SLOTS + 1,), jnp.int32)
KV = pltpu.VMEM((SLOTS, 2, BLOCK, HD), jnp.bfloat16)
TALL = pltpu.VMEM((ROWS, HD), jnp.bfloat16)
FLAT = pltpu.VMEM((HD, ROWS), jnp.bfloat16)
PROBS = pltpu.VMEM((SLOTS, BLOCK, ROWS), jnp.float32)
ACC = pltpu.VMEM((HD, ROWS), jnp.float32)


def forward(order, lens, q, near, far):
    return pl.pallas_call(
        forward_kernel,
        out_shape=WHOLE,
        in_specs=[SMEM, SMEM, VMEM, VMEM, VMEM],
        out_specs=VMEM,
        scratch_shapes=[LIST, LIST, KV, FLAT, PROBS, ACC],
        compiler_params=pltpu.CompilerParams(vmem_limit_bytes=32 << 20),
        cost_estimate=pl.CostEstimate(flops=1 << 30, bytes_accessed=2 << 20, transcendentals=1 << 21),
        name="attend_forward",
    )(order, lens, q, near, far)


def backward(order, lens, q, cotan, near, far):
    return pl.pallas_call(
        backward_kernel,
        out_shape=(WHOLE, HALF, HALF),
        in_specs=[SMEM, SMEM, VMEM, VMEM, VMEM, VMEM],
        out_specs=(VMEM, VMEM, VMEM),
        scratch_shapes=[LIST, LIST, KV, FLAT, FLAT, TALL, TALL, PROBS, ACC, KV],
        compiler_params=pltpu.CompilerParams(vmem_limit_bytes=32 << 20),
        cost_estimate=pl.CostEstimate(flops=7 << 29, bytes_accessed=4 << 20, transcendentals=1 << 21),
        name="attend_backward",
    )(order, lens, q, cotan, near, far)


def along_z(x, distance):
    route = [(i, i // RING * RING + (i + distance) % RING) for i in range(SLOTS)]
    return lax.ppermute(x, "ctx", route)


def other_half(x):
    return lax.ppermute(x, "ctx", [(i, i ^ RING) for i in range(SLOTS)])


def other_section(x, flip):
    route = [(p * SLOTS + i, (1 - p) * SLOTS + (i ^ flip)) for p in range(2) for i in range(SLOTS)]
    return lax.ppermute(x, ("pipe", "ctx"), route)


def gather(block):
    x = block[None]
    below, above = along_z(x, 3), along_z(x, -3)
    lower = along_z(jnp.concatenate([x, below, above]), 1)
    upper = along_z(jnp.concatenate([x, below]), -1)
    near = jnp.concatenate([x, below, above, lower, upper])
    return near, other_half(near)


def add(*terms):
    total = terms[0].astype(jnp.float32)
    for term in terms[1:]:
        total = total + term.astype(jnp.float32)
    return total.astype(jnp.bfloat16)


def scatter(dnear, dfar):
    part = add(other_section(dnear, 0), other_section(dfar, RING))
    low = along_z(part[3:6], -1)
    high = along_z(part[6:8], 1)
    own = add(part[0], low[0], high[0])
    below = along_z(add(part[1], low[1], high[1]), -3)
    above = along_z(add(part[2], low[2]), 3)
    return add(own, below, above)


def shards(fwd_queries, fwd_keyvals, bwd_queries, bwd_keyvals, bwd_cotangent, doc_lengths, block_order):
    near, far = gather(bwd_keyvals[0])
    fnear, ffar = gather(fwd_keyvals[0])
    dq, dnear, dfar = backward(block_order, doc_lengths, bwd_queries, bwd_cotangent, near, far)
    keyval_grad = scatter(dnear, dfar)
    query_grad = lax.ppermute(dq, "pipe", [(0, 1), (1, 0)])
    output = forward(block_order, doc_lengths, fwd_queries, fnear, ffar)
    output = lax.ppermute(output, "pipe", [(0, 1), (1, 0)])
    return output, query_grad, keyval_grad[None]


def solution(mesh):
    placed = (
        P("pipe", "ctx", "tp"),
        P("pipe", None, "ctx", "tp"),
        P("pipe", "ctx", "tp"),
        P("pipe", None, "ctx", "tp"),
        P("pipe", "ctx", "tp"),
        P(),
        P(),
    )
    return jax.shard_map(
        shards,
        mesh=mesh,
        in_specs=placed,
        out_specs=(P("pipe", "ctx", "tp"), P("pipe", "ctx", "tp"), P("pipe", None, "ctx", "tp")),
        check_vma=False,
    )
```

```python
import jax
import jax.numpy as jnp
from jax import lax
from jax.experimental import pallas as pl
from jax.experimental.pallas import tpu as pltpu
from jax.sharding import PartitionSpec as P

HD = 128
BLOCK = 128
GROUP = 8
ROWS = GROUP * BLOCK
WIDE = 2 * BLOCK
SLOTS = 16
PAIRS = 2 * 8 + 2
BEYOND = 1 << 20
EXTRA = 16
PACK = 12
ADD = 12
GRADS = 40
TURN = 12
FORWARD = 12
FINISH = 4
RING = 8
OFFSETS = (0, -3, 3, -1, -4, 2, 1, -2)
SCALE = HD**-0.5
LOG2E = 1.4426950408889634
NEG = -1e30


def prepare(batch, table, slots, sides, bases, first, place):
    me = lax.axis_index("ctx")
    half, z = me // RING, me % RING
    query_bases, leasts = [], []
    for side in range(2):
        owner = (half + side) % 2 * RING + z
        query_base = table[batch, owner] * BLOCK
        at = query_base + lax.broadcasted_iota(jnp.int32, (8, BLOCK), 1)
        start = jnp.zeros((8, BLOCK), jnp.int32)
        least = jnp.int32(0)
        end = jnp.int32(0)
        for i in range(SLOTS, table.shape[1]):
            end = end + table[batch, i]
            start = jnp.where(at >= end, end, start)
            least = jnp.where(query_base >= end, end, least)
        first[side] = start
        place[side] = at
        query_bases.append(query_base)
        leasts.append(least)
    count = jnp.int32(0)
    for side in range(2):
        for slot in range(RING):
            owner = half * RING + (z + (OFFSETS[slot] + RING)) % RING
            base = table[batch, owner] * BLOCK
            slots[count] = slot
            sides[count] = side
            bases[count] = base
            active = (base <= query_bases[side]) & (base + (BLOCK - 1) >= leasts[side])
            count = count + active.astype(jnp.int32)
        slots[count] = 0
        bases[count] = BEYOND
        count = count + count % 2
    return count // 2


def dot(a, b):
    return jnp.dot(a, b, preferred_element_type=jnp.float32)


def add(*terms):
    total = terms[0].astype(jnp.float32)
    for term in terms[1:]:
        total = total + term.astype(jnp.float32)
    return total.astype(jnp.bfloat16)


def turn(ref, flat, tall=None):
    for h in range(GROUP):
        part = ref[0, :, h * HD : (h + 1) * HD]
        flat[:, h * BLOCK : (h + 1) * BLOCK] = part.T
        if tall is not None:
            tall[h * BLOCK : (h + 1) * BLOCK, :] = part


def total_kernel(own, below, above, _, out):
    out[0] = add(own[...], below[...], above[...])


def turn_kernel(q, c, q_far, c_far, _, q_t, c_t, q_rows, c_rows):
    turn(q, q_t.at[0], q_rows.at[0])
    turn(c, c_t.at[0], c_rows.at[0])
    turn(q_far, q_t.at[1], q_rows.at[1])
    turn(c_far, c_t.at[1], c_rows.at[1])


def allowed(i, side, bases, first, place):
    row = bases[i] + lax.broadcasted_iota(jnp.int32, (BLOCK, BLOCK), 0)
    return (row >= first[side, 0:1]) & (row <= place[side, 0:1])


def masked_scores(key, q_t, side, mask, c):
    s = dot(key, q_t[side, :, c * WIDE : (c + 1) * WIDE])
    return [
        jnp.where(mask, s[:, j * BLOCK : (j + 1) * BLOCK], NEG) for j in range(WIDE // BLOCK)
    ]


def fold(x, op):
    return op(x.reshape(x.shape[0] // 8, 8, x.shape[1]), axis=0)


def largest(count, slots, sides, bases, first, place, kv, q_t, scores, tops):
    def body(g, _):
        side = sides[2 * g]
        keys = [kv[slots[2 * g + j], 0] for j in range(2)]
        masks = [allowed(2 * g + j, side, bases, first, place) for j in range(2)]
        for c in range(ROWS // WIDE):
            for j in range(2):
                for k, part in enumerate(masked_scores(keys[j], q_t, side, masks[j], c)):
                    at = slice(c * WIDE + k * BLOCK, c * WIDE + (k + 1) * BLOCK)
                    scores[2 * g + j, :, at] = part
                    tops[side, :, at] = jnp.maximum(tops[side, :, at], fold(part, jnp.max))
        return 0

    lax.fori_loop(0, count, body, 0)
    for side in range(2):
        tops[side] = jnp.broadcast_to(jnp.max(tops[side], axis=0, keepdims=True), (8, ROWS))


def statistics(count, slots, sides, bases, first, place, kv, q_t, c_t, scores, tops, totals, deltas):
    tops[...] = jnp.full(tops.shape, NEG, jnp.float32)
    totals[...] = jnp.zeros(totals.shape, jnp.float32)
    deltas[...] = jnp.zeros(deltas.shape, jnp.float32)

    largest(count, slots, sides, bases, first, place, kv, q_t, scores, tops)

    def sums(g, _):
        side = sides[2 * g]
        values = [kv[slots[2 * g + j], 1] for j in range(2)]
        for c in range(ROWS // WIDE):
            at = slice(c * WIDE, (c + 1) * WIDE)
            for j in range(2):
                p = jnp.exp2((scores[2 * g + j, :, at] - tops[side, 0:1, at]) * (SCALE * LOG2E))
                totals[side, :, at] += fold(p, jnp.sum)
                deltas[side, :, at] += fold(p * dot(values[j], c_t[side, :, at]), jnp.sum)
        return 0

    lax.fori_loop(0, count, sums, 0)
    rows = []
    for side in range(2):
        rows.append(tops[side, 0:1])
        rows.append(jnp.sum(totals[side], axis=0, keepdims=True))
        rows.append(jnp.sum(deltas[side], axis=0, keepdims=True))
    rows.append(jnp.zeros((8 - len(rows), ROWS), jnp.float32))
    return jnp.concatenate(rows, axis=0)


def merge(mine, other, per_side=3):
    merged = []
    for side in range(2):
        a = [mine[side * per_side + r : side * per_side + r + 1, :] for r in range(per_side)]
        b = [other[(1 - side) * per_side + r : (1 - side) * per_side + r + 1, :] for r in range(per_side)]
        top = jnp.maximum(a[0], b[0])
        fa = jnp.exp2((a[0] - top) * (SCALE * LOG2E))
        fb = jnp.exp2((b[0] - top) * (SCALE * LOG2E))
        merged.append([top] + [x * fa + y * fb for x, y in zip(a[1:], b[1:])])
    return merged


def backward_stats_kernel(
    table, q_t, c_t, near, out,
    slots, sides, bases, first, place, scores, tops, totals, deltas,
):
    near = near.at[0]
    count = prepare(0, table, slots, sides, bases, first, place)
    out[...] = statistics(
        count, slots, sides, bases, first, place, near, q_t, c_t, scores, tops, totals, deltas
    )


def thirds(x):
    parts = []
    for _ in range(3):
        part = x.astype(jnp.bfloat16).astype(jnp.float32)
        parts.append(part)
        x = x - part
    return parts


def forward_kernel(
    table, q, q_far, near, _, out, out_far,
    slots, sides, bases, first, place, q_t, scores, tops, totals, acc, turned, probs,
):
    near = near.at[1]
    count = prepare(1, table, slots, sides, bases, first, place)
    turn(q, q_t.at[0])
    turn(q_far, q_t.at[1])
    tops[...] = jnp.full(tops.shape, NEG, jnp.float32)
    totals[...] = jnp.zeros(totals.shape, jnp.float32)
    acc[...] = jnp.zeros_like(acc)
    largest(count, slots, sides, bases, first, place, near, q_t, scores, tops)

    def body(g, _):
        side = sides[2 * g]
        for j in range(2):
            turned[:, j * BLOCK : (j + 1) * BLOCK] = near[slots[2 * g + j], 1].T
        for c in range(ROWS // WIDE):
            at = slice(c * WIDE, (c + 1) * WIDE)
            for j in range(2):
                p = jnp.exp2((scores[2 * g + j, :, at] - tops[side, 0:1, at]) * (SCALE * LOG2E))
                totals[side, :, at] += fold(p, jnp.sum)
                probs[j * BLOCK : (j + 1) * BLOCK, at] = p.astype(jnp.bfloat16)
        acc[side] += dot(turned[...], probs[...])
        return 0

    lax.fori_loop(0, count, body, 0)
    for side, ref in enumerate((out, out_far)):
        total = jnp.sum(totals[side], axis=0, keepdims=True)
        total = jnp.maximum(total, 1e-30)
        inverse = 1.0 / total
        for h in range(GROUP):
            at = slice(h * BLOCK, (h + 1) * BLOCK)
            ref[0, :BLOCK, at] = (acc[side, :, at] * inverse[:, at]).T.astype(jnp.bfloat16)
        logs = tops[side, 0:1] * (SCALE * LOG2E) + jnp.log2(total)
        pad = jnp.zeros((EXTRA - 3, ROWS), jnp.float32)
        ref[0, BLOCK:] = jnp.concatenate(thirds(logs) + [pad], axis=0).astype(jnp.bfloat16)


def add_kernel(keep, low, high, _a, _b, own, below, above):
    own[...] = add(keep[0], low[0], high[0])
    below[...] = add(keep[1], low[1], high[1])
    above[...] = add(keep[2], low[2])


def pack_kernel(x, below, above, three, two):
    for i, ref in enumerate((x, below, above)):
        three[:, i : i + 1] = ref[...]
        if i < 2:
            two[:, i : i + 1] = ref[...]


def finish_kernel(dq, dq_far, a, b, query_grad, output, token):
    token[...] = jnp.zeros(token.shape, token.dtype)
    query_grad[...] = add(dq[...], dq_far[...])
    logs = []
    for ref in (a, b):
        rows = ref[0, BLOCK:].astype(jnp.float32)
        logs.append(rows[0:1] + rows[1:2] + rows[2:3])
    top = jnp.maximum(logs[0], logs[1])
    wa, wb = jnp.exp2(logs[0] - top), jnp.exp2(logs[1] - top)
    inverse = 1.0 / (wa + wb)
    wa, wb = wa * inverse, wb * inverse
    for h in range(GROUP):
        at = slice(h * BLOCK, (h + 1) * BLOCK)
        one = jnp.broadcast_to(wa[:, at], (BLOCK, BLOCK)).T
        two = jnp.broadcast_to(wb[:, at], (BLOCK, BLOCK)).T
        x, y = a[0, :BLOCK, at].astype(jnp.float32), b[0, :BLOCK, at].astype(jnp.float32)
        output[0, :, at] = (x * one + y * two).astype(jnp.bfloat16)


def backward_kernel(
    table, q_t, c_t, q_rows, c_rows, near, mine, other, _, dq, dq_far, keep, low, high,
    slots, sides, bases, first, place, rows, acc, dkv, turned, probs, dscores,
):
    near = near.at[0]
    count = prepare(0, table, slots, sides, bases, first, place)
    for side, (top, total, weighted) in enumerate(merge(mine, other)):
        rows[side, 0:1] = top * (SCALE * LOG2E) + jnp.log2(total)
        rows[side, 1:2] = weighted / total
    acc[...] = jnp.zeros_like(acc)
    dkv[...] = jnp.zeros_like(dkv)

    def grads(g, _):
        side = sides[2 * g]
        for j in range(2):
            at_rows = slice(j * BLOCK, (j + 1) * BLOCK)
            key = near[slots[2 * g + j], 0]
            value = near[slots[2 * g + j], 1]
            mask = allowed(2 * g + j, side, bases, first, place)
            turned[:, at_rows] = key.T
            for c in range(ROWS // WIDE):
                at = slice(c * WIDE, (c + 1) * WIDE)
                s = jnp.concatenate(masked_scores(key, q_t, side, mask, c), axis=1)
                p = jnp.exp2(s * (SCALE * LOG2E) - rows[side, 0:1, at])
                dp = dot(value, c_t[side, :, at])
                probs[at_rows, at] = p.astype(jnp.bfloat16)
                dscores[at_rows, at] = (p * (dp - rows[side, 1:2, at])).astype(jnp.bfloat16)
        dv = dot(probs[...], c_rows[side])
        dk = dot(dscores[...], q_rows[side]) * SCALE
        acc[side] += dot(turned[...], dscores[...])
        for j in range(2):
            at_rows = slice(j * BLOCK, (j + 1) * BLOCK)
            dkv[slots[2 * g + j], 0] += dk[at_rows]
            dkv[slots[2 * g + j], 1] += dv[at_rows]
        return 0

    lax.fori_loop(0, count, grads, 0)
    keep[...] = dkv[0:3].astype(jnp.bfloat16)
    low[...] = dkv[3:6].astype(jnp.bfloat16)
    high[...] = dkv[6:8].astype(jnp.bfloat16)
    for side, ref in enumerate((dq, dq_far)):
        for h in range(GROUP):
            at = slice(h * BLOCK, (h + 1) * BLOCK)
            ref[0, :, at] = (acc[side, :, at] * SCALE).T.astype(jnp.bfloat16)


SMEM = pl.BlockSpec(memory_space=pltpu.SMEM)
VMEM = pl.BlockSpec(memory_space=pltpu.VMEM)
WHOLE = jax.ShapeDtypeStruct((1, BLOCK, GROUP * HD), jnp.bfloat16)
TOKEN = jax.ShapeDtypeStruct((8, 128), jnp.float32)
STATS = jax.ShapeDtypeStruct((8, ROWS), jnp.float32)
LIST = pltpu.SMEM((PAIRS + 1,), jnp.int32)
PLACES = pltpu.VMEM((2, 8, BLOCK), jnp.int32)
LISTS = [LIST, LIST, LIST, PLACES, PLACES]
TALLS = jax.ShapeDtypeStruct((2, ROWS, HD), jnp.bfloat16)
FLATS = jax.ShapeDtypeStruct((2, HD, ROWS), jnp.bfloat16)
FLAT = pltpu.VMEM((2, HD, ROWS), jnp.bfloat16)
PART = jax.ShapeDtypeStruct((2, BLOCK, HD), jnp.bfloat16)
TALLER = jax.ShapeDtypeStruct((1, BLOCK + EXTRA, GROUP * HD), jnp.bfloat16)
SCORES = pltpu.VMEM((PAIRS, BLOCK, ROWS), jnp.float32)
ACC = pltpu.VMEM((2, HD, ROWS), jnp.float32)
TURNED = pltpu.VMEM((HD, 2 * BLOCK), jnp.bfloat16)
PROBS = pltpu.VMEM((2 * BLOCK, ROWS), jnp.bfloat16)
SUMS = pltpu.VMEM((2, 8, ROWS), jnp.float32)
DKV = pltpu.VMEM((RING, 2, BLOCK, HD), jnp.float32)


def blocks(n):
    return jax.ShapeDtypeStruct((n, 2, BLOCK, HD), jnp.bfloat16)


def pairs(n):
    return jax.ShapeDtypeStruct((2, n, 2, BLOCK, HD), jnp.bfloat16)


def kernel(body, name, outs, scratch, cost, args, lists=()):
    single = not isinstance(outs, tuple)
    return pl.pallas_call(
        body,
        out_shape=outs,
        in_specs=[SMEM] * len(lists) + [VMEM] * len(args),
        out_specs=VMEM if single else (VMEM,) * len(outs),
        scratch_shapes=(LISTS if lists else []) + scratch,
        compiler_params=pltpu.CompilerParams(vmem_limit_bytes=32 << 20),
        cost_estimate=pl.CostEstimate(
            flops=cost << 29, bytes_accessed=2 << 20, transcendentals=1 << 21
        ),
        name=name,
    )(*lists, *args)


def along_z(x, distance):
    route = [(i, i // RING * RING + (i + distance) % RING) for i in range(SLOTS)]
    return lax.ppermute(x, "ctx", route)


def across_x(x):
    return lax.ppermute(x, "ctx", [(i, i ^ RING) for i in range(SLOTS)])


def other_section(x, flip=0, distance=0):
    route = [
        (p * SLOTS + i, (1 - p) * SLOTS + (i // RING * RING + (i + distance) % RING ^ flip))
        for p in range(2)
        for i in range(SLOTS)
    ]
    return lax.ppermute(x, ("pipe", "ctx"), route)


def gather(x):
    below, above = along_z(x, 3), along_z(x, -3)
    three, two = kernel(pack_kernel, "pack", (pairs(3), pairs(2)), [], PACK, (x, below, above))
    return jnp.concatenate([three, along_z(three, 1), along_z(two, -1)], axis=1), three


def shards(fwd_queries, fwd_keyvals, bwd_queries, bwd_keyvals, bwd_cotangent, doc_lengths, block_order):
    lists = (jnp.concatenate([block_order, doc_lengths], axis=1),)
    near, three = gather(jnp.stack([bwd_keyvals, fwd_keyvals]))
    q_t, c_t, q_rows, c_rows = kernel(
        turn_kernel, "turn", (FLATS, FLATS, TALLS, TALLS), [], TURN,
        (bwd_queries, bwd_cotangent, across_x(bwd_queries), across_x(bwd_cotangent), three),
    )
    mine = kernel(
        backward_stats_kernel, "backward_stats", STATS,
        [SCORES, SUMS, SUMS, SUMS], 2, (q_t, c_t, near), lists,
    )
    other = across_x(mine)
    out, out_far = kernel(
        forward_kernel, "forward", (TALLER, TALLER),
        [FLAT, SCORES, SUMS, SUMS, ACC, TURNED, PROBS], FORWARD, (fwd_queries, across_x(fwd_queries), near, mine), lists,
    )
    dq, dq_far, keep, low, high = kernel(
        backward_kernel, "backward_grads", (WHOLE, WHOLE, blocks(3), blocks(3), blocks(2)),
        [SUMS, ACC, DKV, TURNED, PROBS, PROBS], GRADS, (q_t, c_t, q_rows, c_rows, near, mine, other, out), lists,
    )
    out, out_far = other_section(out), other_section(out_far, RING)
    low, high = along_z(low, -1), along_z(high, 1)
    dq, dq_far = other_section(dq), other_section(dq_far, RING)
    own, below, above = kernel(
        add_kernel, "add", (PART, PART, PART), [], ADD, (keep, low, high, out, out_far),
    )
    own, below, above = other_section(own), other_section(below, 0, -3), other_section(above, 0, 3)
    query_grad, output, token = kernel(
        finish_kernel, "finish", (WHOLE, WHOLE, TOKEN), [], FINISH, (dq, dq_far, out, out_far)
    )
    keyval_grad = kernel(total_kernel, "total", blocks(1), [], 0, (own, below, above, token))
    return output, query_grad, keyval_grad


def solution(mesh):
    placed = (
        P("pipe", "ctx", "tp"),
        P("pipe", None, "ctx", "tp"),
        P("pipe", "ctx", "tp"),
        P("pipe", None, "ctx", "tp"),
        P("pipe", "ctx", "tp"),
        P(),
        P(),
    )
    return jax.shard_map(
        shards,
        mesh=mesh,
        in_specs=placed,
        out_specs=(P("pipe", "ctx", "tp"), P("pipe", "ctx", "tp"), P("pipe", None, "ctx", "tp")),
        check_vma=False,
    )
```

```python
import jax
import jax.numpy as jnp
from jax import lax
from jax.experimental import pallas as pl
from jax.experimental.pallas import tpu as pltpu
from jax.sharding import PartitionSpec as P

HD = 128
BLOCK = 128
GROUP = 8
ROWS = GROUP * BLOCK
WIDE = 2 * BLOCK
SLOTS = 16
PAIRS = 2 * 8 + 2
BEYOND = 1 << 20
EXTRA = 16
FINAL = 128 + EXTRA
PACK = 12
HOLD = 0
ADD = 12
GRADS = 40
TURN = 12
FORWARD = 12
FINISH = 4
RING = 8
OFFSETS = (0, -3, 3, -1, -4, 2, 1, -2)
SCALE = HD**-0.5
LOG2E = 1.4426950408889634
NEG = -1e30


def prepare(batch, table, slots, sides, bases, first, place):
    me = lax.axis_index("ctx")
    half, z = me // RING, me % RING
    query_bases, leasts = [], []
    for side in range(2):
        owner = (half + side) % 2 * RING + z
        query_base = table[batch, owner] * BLOCK
        at = query_base + lax.broadcasted_iota(jnp.int32, (8, BLOCK), 1)
        start = jnp.zeros((8, BLOCK), jnp.int32)
        least = jnp.int32(0)
        end = jnp.int32(0)
        for i in range(SLOTS, table.shape[1]):
            end = end + table[batch, i]
            start = jnp.where(at >= end, end, start)
            least = jnp.where(query_base >= end, end, least)
        first[side] = start
        place[side] = at
        query_bases.append(query_base)
        leasts.append(least)
    count = jnp.int32(0)
    for side in range(2):
        for slot in range(RING):
            owner = half * RING + (z + (OFFSETS[slot] + RING)) % RING
            base = table[batch, owner] * BLOCK
            slots[count] = slot
            sides[count] = side
            bases[count] = base
            active = (base <= query_bases[side]) & (base + (BLOCK - 1) >= leasts[side])
            count = count + active.astype(jnp.int32)
        slots[count] = 0
        bases[count] = BEYOND
        count = count + count % 2
    return count // 2


def dot(a, b):
    return jnp.dot(a, b, preferred_element_type=jnp.float32)


def add(*terms):
    total = terms[0].astype(jnp.float32)
    for term in terms[1:]:
        total = total + term.astype(jnp.float32)
    return total.astype(jnp.bfloat16)


def turn(ref, flat, tall=None):
    for h in range(GROUP):
        part = ref[0, :, h * HD : (h + 1) * HD]
        flat[:, h * BLOCK : (h + 1) * BLOCK] = part.T
        if tall is not None:
            tall[h * BLOCK : (h + 1) * BLOCK, :] = part


def total_kernel(own, below, above, _, out):
    out[0] = add(own[...], below[...], above[...])


def turn_kernel(q, c, q_far, c_far, later, _, q_t, c_t, q_rows, c_rows, held):
    held[...] = later[...]
    turn(q, q_t.at[0], q_rows.at[0])
    turn(c, c_t.at[0], c_rows.at[0])
    turn(q_far, q_t.at[1], q_rows.at[1])
    turn(c_far, c_t.at[1], c_rows.at[1])


def allowed(i, side, bases, first, place):
    row = bases[i] + lax.broadcasted_iota(jnp.int32, (BLOCK, BLOCK), 0)
    return (row >= first[side, 0:1]) & (row <= place[side, 0:1])


def masked_scores(key, q_t, side, mask, c):
    s = dot(key, q_t[side, :, c * WIDE : (c + 1) * WIDE])
    return [
        jnp.where(mask, s[:, j * BLOCK : (j + 1) * BLOCK], NEG) for j in range(WIDE // BLOCK)
    ]


def fold(x, op):
    return op(x.reshape(x.shape[0] // 8, 8, x.shape[1]), axis=0)


def largest(count, slots, sides, bases, first, place, kv, q_t, scores, tops):
    def body(g, _):
        side = sides[2 * g]
        keys = [kv[slots[2 * g + j], 0] for j in range(2)]
        masks = [allowed(2 * g + j, side, bases, first, place) for j in range(2)]
        for c in range(ROWS // WIDE):
            for j in range(2):
                for k, part in enumerate(masked_scores(keys[j], q_t, side, masks[j], c)):
                    at = slice(c * WIDE + k * BLOCK, c * WIDE + (k + 1) * BLOCK)
                    scores[2 * g + j, :, at] = part
                    tops[side, :, at] = jnp.maximum(tops[side, :, at], fold(part, jnp.max))
        return 0

    lax.fori_loop(0, count, body, 0)
    for side in range(2):
        tops[side] = jnp.broadcast_to(jnp.max(tops[side], axis=0, keepdims=True), (8, ROWS))


def statistics(count, slots, sides, bases, first, place, kv, q_t, c_t, scores, tops, totals, deltas):
    tops[...] = jnp.full(tops.shape, NEG, jnp.float32)
    totals[...] = jnp.zeros(totals.shape, jnp.float32)
    deltas[...] = jnp.zeros(deltas.shape, jnp.float32)

    largest(count, slots, sides, bases, first, place, kv, q_t, scores, tops)

    def sums(g, _):
        side = sides[2 * g]
        values = [kv[slots[2 * g + j], 1] for j in range(2)]
        for c in range(ROWS // WIDE):
            at = slice(c * WIDE, (c + 1) * WIDE)
            for j in range(2):
                p = jnp.exp2((scores[2 * g + j, :, at] - tops[side, 0:1, at]) * (SCALE * LOG2E))
                totals[side, :, at] += fold(p, jnp.sum)
                deltas[side, :, at] += fold(p * dot(values[j], c_t[side, :, at]), jnp.sum)
        return 0

    lax.fori_loop(0, count, sums, 0)
    rows = []
    for side in range(2):
        rows.append(tops[side, 0:1])
        rows.append(jnp.sum(totals[side], axis=0, keepdims=True))
        rows.append(jnp.sum(deltas[side], axis=0, keepdims=True))
    rows.append(jnp.zeros((8 - len(rows), ROWS), jnp.float32))
    return jnp.concatenate(rows, axis=0)


def merge(mine, other, per_side=3):
    merged = []
    for side in range(2):
        a = [mine[side * per_side + r : side * per_side + r + 1, :] for r in range(per_side)]
        b = [other[(1 - side) * per_side + r : (1 - side) * per_side + r + 1, :] for r in range(per_side)]
        top = jnp.maximum(a[0], b[0])
        fa = jnp.exp2((a[0] - top) * (SCALE * LOG2E))
        fb = jnp.exp2((b[0] - top) * (SCALE * LOG2E))
        merged.append([top] + [x * fa + y * fb for x, y in zip(a[1:], b[1:])])
    return merged


def backward_stats_kernel(
    table, q_t, c_t, near, out,
    slots, sides, bases, first, place, scores, tops, totals, deltas,
):
    count = prepare(0, table, slots, sides, bases, first, place)
    out[...] = statistics(
        count, slots, sides, bases, first, place, near, q_t, c_t, scores, tops, totals, deltas
    )


def thirds(x):
    parts = []
    for _ in range(3):
        part = x.astype(jnp.bfloat16).astype(jnp.float32)
        parts.append(part)
        x = x - part
    return parts


def forward_kernel(
    table, q, q_far, near, dq, dq_far, out, out_far,
    slots, sides, bases, first, place, q_t, scores, tops, totals, acc, turned, probs,
):
    count = prepare(1, table, slots, sides, bases, first, place)
    turn(q, q_t.at[0])
    turn(q_far, q_t.at[1])
    tops[...] = jnp.full(tops.shape, NEG, jnp.float32)
    totals[...] = jnp.zeros(totals.shape, jnp.float32)
    acc[...] = jnp.zeros_like(acc)
    largest(count, slots, sides, bases, first, place, near, q_t, scores, tops)

    def body(g, _):
        side = sides[2 * g]
        for j in range(2):
            turned[:, j * BLOCK : (j + 1) * BLOCK] = near[slots[2 * g + j], 1].T
        for c in range(ROWS // WIDE):
            at = slice(c * WIDE, (c + 1) * WIDE)
            for j in range(2):
                p = jnp.exp2((scores[2 * g + j, :, at] - tops[side, 0:1, at]) * (SCALE * LOG2E))
                totals[side, :, at] += fold(p, jnp.sum)
                probs[j * BLOCK : (j + 1) * BLOCK, at] = p.astype(jnp.bfloat16)
        acc[side] += dot(turned[...], probs[...])
        return 0

    lax.fori_loop(0, count, body, 0)
    for side, (ref, grad) in enumerate(((out, dq), (out_far, dq_far))):
        ref[0, FINAL:] = grad[0]
        total = jnp.sum(totals[side], axis=0, keepdims=True)
        total = jnp.maximum(total, 1e-30)
        inverse = 1.0 / total
        for h in range(GROUP):
            at = slice(h * BLOCK, (h + 1) * BLOCK)
            ref[0, :BLOCK, at] = (acc[side, :, at] * inverse[:, at]).T.astype(jnp.bfloat16)
        logs = tops[side, 0:1] * (SCALE * LOG2E) + jnp.log2(total)
        pad = jnp.zeros((EXTRA - 3, ROWS), jnp.float32)
        ref[0, BLOCK:FINAL] = jnp.concatenate(thirds(logs) + [pad], axis=0).astype(jnp.bfloat16)


def add_kernel(keep, low, high, _, own, below, above):
    own[...] = add(keep[0], low[0], high[0])
    below[...] = add(keep[1], low[1], high[1])
    above[...] = add(keep[2], low[2])


def pack_kernel(x, below, above, _, three, two):
    for i, ref in enumerate((x, below, above)):
        three[i] = ref[0]
        if i < 2:
            two[i] = ref[0]


def hold_kernel(x, _, out):
    out[...] = x[...]


def finish_kernel(a, b, query_grad, output, token):
    token[...] = jnp.zeros(token.shape, token.dtype)
    query_grad[0] = add(a[0, FINAL:], b[0, FINAL:])
    logs = []
    for ref in (a, b):
        rows = ref[0, BLOCK:FINAL].astype(jnp.float32)
        logs.append(rows[0:1] + rows[1:2] + rows[2:3])
    top = jnp.maximum(logs[0], logs[1])
    wa, wb = jnp.exp2(logs[0] - top), jnp.exp2(logs[1] - top)
    inverse = 1.0 / (wa + wb)
    wa, wb = wa * inverse, wb * inverse
    for h in range(GROUP):
        at = slice(h * BLOCK, (h + 1) * BLOCK)
        one = jnp.broadcast_to(wa[:, at], (BLOCK, BLOCK)).T
        two = jnp.broadcast_to(wb[:, at], (BLOCK, BLOCK)).T
        x, y = a[0, :BLOCK, at].astype(jnp.float32), b[0, :BLOCK, at].astype(jnp.float32)
        output[0, :, at] = (x * one + y * two).astype(jnp.bfloat16)


def backward_kernel(
    table, q_t, c_t, q_rows, c_rows, near, mine, other, dq, dq_far, keep, low, high,
    slots, sides, bases, first, place, rows, acc, dkv, turned, probs, dscores,
):
    count = prepare(0, table, slots, sides, bases, first, place)
    for side, (top, total, weighted) in enumerate(merge(mine, other)):
        rows[side, 0:1] = top * (SCALE * LOG2E) + jnp.log2(total)
        rows[side, 1:2] = weighted / total
    acc[...] = jnp.zeros_like(acc)
    dkv[...] = jnp.zeros_like(dkv)

    def grads(g, _):
        side = sides[2 * g]
        for j in range(2):
            at_rows = slice(j * BLOCK, (j + 1) * BLOCK)
            key = near[slots[2 * g + j], 0]
            value = near[slots[2 * g + j], 1]
            mask = allowed(2 * g + j, side, bases, first, place)
            turned[:, at_rows] = key.T
            for c in range(ROWS // WIDE):
                at = slice(c * WIDE, (c + 1) * WIDE)
                s = jnp.concatenate(masked_scores(key, q_t, side, mask, c), axis=1)
                p = jnp.exp2(s * (SCALE * LOG2E) - rows[side, 0:1, at])
                dp = dot(value, c_t[side, :, at])
                probs[at_rows, at] = p.astype(jnp.bfloat16)
                dscores[at_rows, at] = (p * (dp - rows[side, 1:2, at])).astype(jnp.bfloat16)
        dv = dot(probs[...], c_rows[side])
        dk = dot(dscores[...], q_rows[side]) * SCALE
        acc[side] += dot(turned[...], dscores[...])
        for j in range(2):
            at_rows = slice(j * BLOCK, (j + 1) * BLOCK)
            dkv[slots[2 * g + j], 0] += dk[at_rows]
            dkv[slots[2 * g + j], 1] += dv[at_rows]
        return 0

    lax.fori_loop(0, count, grads, 0)
    keep[...] = dkv[0:3].astype(jnp.bfloat16)
    low[...] = dkv[3:6].astype(jnp.bfloat16)
    high[...] = dkv[6:8].astype(jnp.bfloat16)
    for side, ref in enumerate((dq, dq_far)):
        for h in range(GROUP):
            at = slice(h * BLOCK, (h + 1) * BLOCK)
            ref[0, :, at] = (acc[side, :, at] * SCALE).T.astype(jnp.bfloat16)


SMEM = pl.BlockSpec(memory_space=pltpu.SMEM)
VMEM = pl.BlockSpec(memory_space=pltpu.VMEM)
WHOLE = jax.ShapeDtypeStruct((1, BLOCK, GROUP * HD), jnp.bfloat16)
TOKEN = jax.ShapeDtypeStruct((8, 128), jnp.float32)
STATS = jax.ShapeDtypeStruct((8, ROWS), jnp.float32)
LIST = pltpu.SMEM((PAIRS + 1,), jnp.int32)
PLACES = pltpu.VMEM((2, 8, BLOCK), jnp.int32)
LISTS = [LIST, LIST, LIST, PLACES, PLACES]
TALLS = jax.ShapeDtypeStruct((2, ROWS, HD), jnp.bfloat16)
FLATS = jax.ShapeDtypeStruct((2, HD, ROWS), jnp.bfloat16)
FLAT = pltpu.VMEM((2, HD, ROWS), jnp.bfloat16)
PART = jax.ShapeDtypeStruct((2, BLOCK, HD), jnp.bfloat16)
TALLER = jax.ShapeDtypeStruct((1, FINAL + BLOCK, GROUP * HD), jnp.bfloat16)
SCORES = pltpu.VMEM((PAIRS, BLOCK, ROWS), jnp.float32)
ACC = pltpu.VMEM((2, HD, ROWS), jnp.float32)
TURNED = pltpu.VMEM((HD, 2 * BLOCK), jnp.bfloat16)
PROBS = pltpu.VMEM((2 * BLOCK, ROWS), jnp.bfloat16)
SUMS = pltpu.VMEM((2, 8, ROWS), jnp.float32)
DKV = pltpu.VMEM((RING, 2, BLOCK, HD), jnp.float32)


def blocks(n):
    return jax.ShapeDtypeStruct((n, 2, BLOCK, HD), jnp.bfloat16)


def kernel(body, name, outs, scratch, cost, args, lists=()):
    single = not isinstance(outs, tuple)
    return pl.pallas_call(
        body,
        out_shape=outs,
        in_specs=[SMEM] * len(lists) + [VMEM] * len(args),
        out_specs=VMEM if single else (VMEM,) * len(outs),
        scratch_shapes=(LISTS if lists else []) + scratch,
        compiler_params=pltpu.CompilerParams(vmem_limit_bytes=32 << 20),
        cost_estimate=pl.CostEstimate(
            flops=cost << 29, bytes_accessed=2 << 20, transcendentals=1 << 21
        ),
        name=name,
    )(*lists, *args)


def along_z(x, distance):
    route = [(i, i // RING * RING + (i + distance) % RING) for i in range(SLOTS)]
    return lax.ppermute(x, "ctx", route)


def across_x(x):
    return lax.ppermute(x, "ctx", [(i, i ^ RING) for i in range(SLOTS)])


def other_section(x, flip=0, distance=0):
    route = [
        (p * SLOTS + i, (1 - p) * SLOTS + (i // RING * RING + (i + distance) % RING ^ flip))
        for p in range(2)
        for i in range(SLOTS)
    ]
    return lax.ppermute(x, ("pipe", "ctx"), route)


def hold(x, after):
    return kernel(hold_kernel, "hold", jax.ShapeDtypeStruct(x.shape, x.dtype), [], HOLD, (x, after))


def gather(x, after):
    below, above = along_z(x, 3), along_z(x, -3)
    three, two = kernel(pack_kernel, "pack", (blocks(3), blocks(2)), [], PACK, (x, below, above, after))
    return jnp.concatenate([three, along_z(three, 1), along_z(two, -1)]), three


def shards(fwd_queries, fwd_keyvals, bwd_queries, bwd_keyvals, bwd_cotangent, doc_lengths, block_order):
    lists = (jnp.concatenate([block_order, doc_lengths], axis=1),)
    near, three = gather(bwd_keyvals, bwd_keyvals)
    q_t, c_t, q_rows, c_rows, held = kernel(
        turn_kernel, "turn", (FLATS, FLATS, TALLS, TALLS, WHOLE), [], TURN,
        (bwd_queries, bwd_cotangent, across_x(bwd_queries), across_x(bwd_cotangent), fwd_queries, three),
    )
    mine = kernel(
        backward_stats_kernel, "backward_stats", STATS,
        [SCORES, SUMS, SUMS, SUMS], 2, (q_t, c_t, near), lists,
    )
    other = across_x(mine)
    dq, dq_far, keep, low, high = kernel(
        backward_kernel, "backward_grads", (WHOLE, WHOLE, blocks(3), blocks(3), blocks(2)),
        [SUMS, ACC, DKV, TURNED, PROBS, PROBS], GRADS, (q_t, c_t, q_rows, c_rows, near, mine, other), lists,
    )
    low, high = along_z(low, -1), along_z(high, 1)
    near_later, _ = gather(hold(fwd_keyvals, three), mine)
    held = hold(held, mine)
    out, out_far = kernel(
        forward_kernel, "forward", (TALLER, TALLER),
        [FLAT, SCORES, SUMS, SUMS, ACC, TURNED, PROBS], FORWARD, (held, across_x(held), near_later, dq, dq_far), lists,
    )
    own, below, above = kernel(
        add_kernel, "add", (PART, PART, PART), [], ADD, (keep, low, high, out),
    )
    out, out_far = other_section(out), other_section(out_far, RING)
    own, below, above = other_section(own), other_section(below, 0, -3), other_section(above, 0, 3)
    query_grad, output, token = kernel(
        finish_kernel, "finish", (WHOLE, WHOLE, TOKEN), [], FINISH, (out, out_far)
    )
    keyval_grad = kernel(
        total_kernel, "total", blocks(1), [], 0, (own, below, above, token)
    )
    return output, query_grad, keyval_grad


def solution(mesh):
    placed = (
        P("pipe", "ctx", "tp"),
        P("pipe", None, "ctx", "tp"),
        P("pipe", "ctx", "tp"),
        P("pipe", None, "ctx", "tp"),
        P("pipe", "ctx", "tp"),
        P(),
        P(),
    )
    return jax.shard_map(
        shards,
        mesh=mesh,
        in_specs=placed,
        out_specs=(P("pipe", "ctx", "tp"), P("pipe", "ctx", "tp"), P("pipe", None, "ctx", "tp")),
        check_vma=False,
    )
```

```python
import jax
import jax.numpy as jnp
from jax import lax
from jax.experimental import pallas as pl
from jax.experimental.pallas import tpu as pltpu
from jax.sharding import PartitionSpec as P

HD = 128
BLOCK = 128
GROUP = 8
ROWS = GROUP * BLOCK
WIDE = 2 * BLOCK
SLOTS = 16
PAIRS = 2 * 8 + 2
BEYOND = 1 << 20
EXTRA = 16
FINAL = 128 + EXTRA
PACK = 12
HOLD = 0
ADD = 12
GRADS = 40
TURN = 12
FORWARD = 12
FINISH = 4
RING = 8
OFFSETS = (0, -3, 3, -1, -4, 2, 1, -2)
SCALE = HD**-0.5
LOG2E = 1.4426950408889634
NEG = -1e30


def prepare(batch, table, slots, sides, bases, first, place):
    me = lax.axis_index("ctx")
    half, z = me // RING, me % RING
    query_bases, leasts = [], []
    for side in range(2):
        owner = (half + side) % 2 * RING + z
        query_base = table[batch, owner] * BLOCK
        at = query_base + lax.broadcasted_iota(jnp.int32, (8, BLOCK), 1)
        start = jnp.zeros((8, BLOCK), jnp.int32)
        least = jnp.int32(0)
        end = jnp.int32(0)
        for i in range(SLOTS, table.shape[1]):
            end = end + table[batch, i]
            start = jnp.where(at >= end, end, start)
            least = jnp.where(query_base >= end, end, least)
        first[side] = start
        place[side] = at
        query_bases.append(query_base)
        leasts.append(least)
    count = jnp.int32(0)
    for side in range(2):
        for slot in range(RING):
            owner = half * RING + (z + (OFFSETS[slot] + RING)) % RING
            base = table[batch, owner] * BLOCK
            slots[count] = slot
            sides[count] = side
            bases[count] = base
            active = (base <= query_bases[side]) & (base + (BLOCK - 1) >= leasts[side])
            count = count + active.astype(jnp.int32)
        slots[count] = 0
        bases[count] = BEYOND
        count = count + count % 2
    return count // 2


def dot(a, b):
    return jnp.dot(a, b, preferred_element_type=jnp.float32)


def add(*terms):
    total = terms[0].astype(jnp.float32)
    for term in terms[1:]:
        total = total + term.astype(jnp.float32)
    return total.astype(jnp.bfloat16)


def turn(ref, flat, tall=None):
    for h in range(GROUP):
        part = ref[0, :, h * HD : (h + 1) * HD]
        flat[:, h * BLOCK : (h + 1) * BLOCK] = part.T
        if tall is not None:
            tall[h * BLOCK : (h + 1) * BLOCK, :] = part


def total_kernel(own, below, above, _, out):
    out[0] = add(own[...], below[...], above[...])


def turn_kernel(q, c, q_far, c_far, later, _, q_t, c_t, q_rows, c_rows, held):
    turn(later, held.at[0])
    turn(q, q_t.at[0], q_rows.at[0])
    turn(c, c_t.at[0], c_rows.at[0])
    turn(q_far, q_t.at[1], q_rows.at[1])
    turn(c_far, c_t.at[1], c_rows.at[1])


def allowed(i, side, bases, first, place):
    row = bases[i] + lax.broadcasted_iota(jnp.int32, (BLOCK, BLOCK), 0)
    return (row >= first[side, 0:1]) & (row <= place[side, 0:1])


def masked_scores(key, q_t, side, mask, c):
    s = dot(key, q_t[side, :, c * WIDE : (c + 1) * WIDE])
    return [
        jnp.where(mask, s[:, j * BLOCK : (j + 1) * BLOCK], NEG) for j in range(WIDE // BLOCK)
    ]


def fold(x, op):
    return op(x.reshape(x.shape[0] // 8, 8, x.shape[1]), axis=0)


def largest(count, slots, sides, bases, first, place, kv, q_t, scores, tops):
    def body(g, _):
        side = sides[2 * g]
        keys = [kv[slots[2 * g + j], 0] for j in range(2)]
        masks = [allowed(2 * g + j, side, bases, first, place) for j in range(2)]
        for c in range(ROWS // WIDE):
            for j in range(2):
                for k, part in enumerate(masked_scores(keys[j], q_t, side, masks[j], c)):
                    at = slice(c * WIDE + k * BLOCK, c * WIDE + (k + 1) * BLOCK)
                    scores[2 * g + j, :, at] = part
                    tops[side, :, at] = jnp.maximum(tops[side, :, at], fold(part, jnp.max))
        return 0

    lax.fori_loop(0, count, body, 0)
    for side in range(2):
        tops[side] = jnp.broadcast_to(jnp.max(tops[side], axis=0, keepdims=True), (8, ROWS))


def statistics(count, slots, sides, bases, first, place, kv, q_t, c_t, scores, tops, totals, deltas):
    tops[...] = jnp.full(tops.shape, NEG, jnp.float32)
    totals[...] = jnp.zeros(totals.shape, jnp.float32)
    deltas[...] = jnp.zeros(deltas.shape, jnp.float32)

    largest(count, slots, sides, bases, first, place, kv, q_t, scores, tops)

    def sums(g, _):
        side = sides[2 * g]
        values = [kv[slots[2 * g + j], 1] for j in range(2)]
        for c in range(ROWS // WIDE):
            at = slice(c * WIDE, (c + 1) * WIDE)
            for j in range(2):
                p = jnp.exp2((scores[2 * g + j, :, at] - tops[side, 0:1, at]) * (SCALE * LOG2E))
                totals[side, :, at] += fold(p, jnp.sum)
                deltas[side, :, at] += fold(p * dot(values[j], c_t[side, :, at]), jnp.sum)
        return 0

    lax.fori_loop(0, count, sums, 0)
    rows = []
    for side in range(2):
        rows.append(tops[side, 0:1])
        rows.append(jnp.sum(totals[side], axis=0, keepdims=True))
        rows.append(jnp.sum(deltas[side], axis=0, keepdims=True))
    rows.append(jnp.zeros((8 - len(rows), ROWS), jnp.float32))
    return jnp.concatenate(rows, axis=0)


def merge(mine, other, per_side=3):
    merged = []
    for side in range(2):
        a = [mine[side * per_side + r : side * per_side + r + 1, :] for r in range(per_side)]
        b = [other[(1 - side) * per_side + r : (1 - side) * per_side + r + 1, :] for r in range(per_side)]
        top = jnp.maximum(a[0], b[0])
        fa = jnp.exp2((a[0] - top) * (SCALE * LOG2E))
        fb = jnp.exp2((b[0] - top) * (SCALE * LOG2E))
        merged.append([top] + [x * fa + y * fb for x, y in zip(a[1:], b[1:])])
    return merged


def backward_stats_kernel(
    table, q_t, c_t, near, out,
    slots, sides, bases, first, place, scores, tops, totals, deltas,
):
    count = prepare(0, table, slots, sides, bases, first, place)
    out[...] = statistics(
        count, slots, sides, bases, first, place, near, q_t, c_t, scores, tops, totals, deltas
    )


def thirds(x):
    parts = []
    for _ in range(3):
        part = x.astype(jnp.bfloat16).astype(jnp.float32)
        parts.append(part)
        x = x - part
    return parts


def forward_kernel(
    table, q, q_far, near, dq, dq_far, out, out_far,
    slots, sides, bases, first, place, q_t, scores, tops, totals, acc, turned, probs,
):
    count = prepare(1, table, slots, sides, bases, first, place)
    q_t[0], q_t[1] = q[0], q_far[0]
    tops[...] = jnp.full(tops.shape, NEG, jnp.float32)
    totals[...] = jnp.zeros(totals.shape, jnp.float32)
    acc[...] = jnp.zeros_like(acc)
    largest(count, slots, sides, bases, first, place, near, q_t, scores, tops)

    def body(g, _):
        side = sides[2 * g]
        for j in range(2):
            turned[:, j * BLOCK : (j + 1) * BLOCK] = near[slots[2 * g + j], 1].T
        for c in range(ROWS // WIDE):
            at = slice(c * WIDE, (c + 1) * WIDE)
            for j in range(2):
                p = jnp.exp2((scores[2 * g + j, :, at] - tops[side, 0:1, at]) * (SCALE * LOG2E))
                totals[side, :, at] += fold(p, jnp.sum)
                probs[j * BLOCK : (j + 1) * BLOCK, at] = p.astype(jnp.bfloat16)
        acc[side] += dot(turned[...], probs[...])
        return 0

    lax.fori_loop(0, count, body, 0)
    for side, (ref, grad) in enumerate(((out, dq), (out_far, dq_far))):
        ref[0, FINAL:] = grad[0]
        total = jnp.sum(totals[side], axis=0, keepdims=True)
        total = jnp.maximum(total, 1e-30)
        ref[0, :HD] = (acc[side] * (1.0 / total)).astype(jnp.bfloat16)
        logs = tops[side, 0:1] * (SCALE * LOG2E) + jnp.log2(total)
        pad = jnp.zeros((EXTRA - 3, ROWS), jnp.float32)
        ref[0, HD:FINAL] = jnp.concatenate(thirds(logs) + [pad], axis=0).astype(jnp.bfloat16)


def add_kernel(keep, low, high, _, own, below, above):
    own[...] = add(keep[0], low[0], high[0])
    below[...] = add(keep[1], low[1], high[1])
    above[...] = add(keep[2], low[2])


def pack_kernel(x, below, above, three, two, three_later, two_later):
    for batch, (wide, narrow) in enumerate(((three, two), (three_later, two_later))):
        for i, ref in enumerate((x, below, above)):
            wide[i] = ref[batch, 0]
            if i < 2:
                narrow[i] = ref[batch, 0]


def hold_kernel(x, _, out):
    out[...] = x[...]


def finish_kernel(a, b, query_grad, output, token):
    token[...] = jnp.zeros(token.shape, token.dtype)
    logs = []
    for ref in (a, b):
        rows = ref[0, HD:FINAL].astype(jnp.float32)
        logs.append(rows[0:1] + rows[1:2] + rows[2:3])
    top = jnp.maximum(logs[0], logs[1])
    wa, wb = jnp.exp2(logs[0] - top), jnp.exp2(logs[1] - top)
    inverse = 1.0 / (wa + wb)
    wa, wb = wa * inverse, wb * inverse
    for h in range(GROUP):
        at = slice(h * BLOCK, (h + 1) * BLOCK)
        x, y = a[0, :HD, at].astype(jnp.float32), b[0, :HD, at].astype(jnp.float32)
        output[0, :, at] = (x * wa[:, at] + y * wb[:, at]).astype(jnp.bfloat16).T
        query_grad[0, :, at] = add(a[0, FINAL:, at], b[0, FINAL:, at]).T


def backward_kernel(
    table, q_t, c_t, q_rows, c_rows, near, mine, other, dq, dq_far, keep, low, high,
    slots, sides, bases, first, place, rows, acc, dkv, turned, probs, dscores,
):
    count = prepare(0, table, slots, sides, bases, first, place)
    for side, (top, total, weighted) in enumerate(merge(mine, other)):
        rows[side, 0:1] = top * (SCALE * LOG2E) + jnp.log2(total)
        rows[side, 1:2] = weighted / total
    acc[...] = jnp.zeros_like(acc)
    dkv[...] = jnp.zeros_like(dkv)

    def grads(g, _):
        side = sides[2 * g]
        for j in range(2):
            at_rows = slice(j * BLOCK, (j + 1) * BLOCK)
            key = near[slots[2 * g + j], 0]
            value = near[slots[2 * g + j], 1]
            mask = allowed(2 * g + j, side, bases, first, place)
            turned[:, at_rows] = key.T
            for c in range(ROWS // WIDE):
                at = slice(c * WIDE, (c + 1) * WIDE)
                s = jnp.concatenate(masked_scores(key, q_t, side, mask, c), axis=1)
                p = jnp.exp2(s * (SCALE * LOG2E) - rows[side, 0:1, at])
                dp = dot(value, c_t[side, :, at])
                probs[at_rows, at] = p.astype(jnp.bfloat16)
                dscores[at_rows, at] = (p * (dp - rows[side, 1:2, at])).astype(jnp.bfloat16)
        dv = dot(probs[...], c_rows[side])
        dk = dot(dscores[...], q_rows[side]) * SCALE
        acc[side] += dot(turned[...], dscores[...])
        for j in range(2):
            at_rows = slice(j * BLOCK, (j + 1) * BLOCK)
            dkv[slots[2 * g + j], 0] += dk[at_rows]
            dkv[slots[2 * g + j], 1] += dv[at_rows]
        return 0

    lax.fori_loop(0, count, grads, 0)
    keep[...] = dkv[0:3].astype(jnp.bfloat16)
    low[...] = dkv[3:6].astype(jnp.bfloat16)
    high[...] = dkv[6:8].astype(jnp.bfloat16)
    for side, ref in enumerate((dq, dq_far)):
        ref[0] = (acc[side] * SCALE).astype(jnp.bfloat16)


SMEM = pl.BlockSpec(memory_space=pltpu.SMEM)
VMEM = pl.BlockSpec(memory_space=pltpu.VMEM)
WHOLE = jax.ShapeDtypeStruct((1, BLOCK, GROUP * HD), jnp.bfloat16)
TOKEN = jax.ShapeDtypeStruct((8, 128), jnp.float32)
STATS = jax.ShapeDtypeStruct((8, ROWS), jnp.float32)
LIST = pltpu.SMEM((PAIRS + 1,), jnp.int32)
PLACES = pltpu.VMEM((2, 8, BLOCK), jnp.int32)
LISTS = [LIST, LIST, LIST, PLACES, PLACES]
TALLS = jax.ShapeDtypeStruct((2, ROWS, HD), jnp.bfloat16)
FLAT1 = jax.ShapeDtypeStruct((1, HD, ROWS), jnp.bfloat16)
FLATS = jax.ShapeDtypeStruct((2, HD, ROWS), jnp.bfloat16)
FLAT = pltpu.VMEM((2, HD, ROWS), jnp.bfloat16)
PART = jax.ShapeDtypeStruct((2, BLOCK, HD), jnp.bfloat16)
TALLER = jax.ShapeDtypeStruct((1, FINAL + BLOCK, GROUP * HD), jnp.bfloat16)
SCORES = pltpu.VMEM((PAIRS, BLOCK, ROWS), jnp.float32)
ACC = pltpu.VMEM((2, HD, ROWS), jnp.float32)
TURNED = pltpu.VMEM((HD, 2 * BLOCK), jnp.bfloat16)
PROBS = pltpu.VMEM((2 * BLOCK, ROWS), jnp.bfloat16)
SUMS = pltpu.VMEM((2, 8, ROWS), jnp.float32)
DKV = pltpu.VMEM((RING, 2, BLOCK, HD), jnp.float32)


def blocks(n):
    return jax.ShapeDtypeStruct((n, 2, BLOCK, HD), jnp.bfloat16)


def kernel(body, name, outs, scratch, cost, args, lists=()):
    single = not isinstance(outs, tuple)
    return pl.pallas_call(
        body,
        out_shape=outs,
        in_specs=[SMEM] * len(lists) + [VMEM] * len(args),
        out_specs=VMEM if single else (VMEM,) * len(outs),
        scratch_shapes=(LISTS if lists else []) + scratch,
        compiler_params=pltpu.CompilerParams(vmem_limit_bytes=32 << 20),
        cost_estimate=pl.CostEstimate(
            flops=cost << 29, bytes_accessed=2 << 20, transcendentals=1 << 21
        ),
        name=name,
    )(*lists, *args)


def along_z(x, distance):
    route = [(i, i // RING * RING + (i + distance) % RING) for i in range(SLOTS)]
    return lax.ppermute(x, "ctx", route)


def across_x(x):
    return lax.ppermute(x, "ctx", [(i, i ^ RING) for i in range(SLOTS)])


def other_section(x, flip=0, distance=0):
    route = [
        (p * SLOTS + i, (1 - p) * SLOTS + (i // RING * RING + (i + distance) % RING ^ flip))
        for p in range(2)
        for i in range(SLOTS)
    ]
    return lax.ppermute(x, ("pipe", "ctx"), route)


def hold(x, after):
    return kernel(hold_kernel, "hold", jax.ShapeDtypeStruct(x.shape, x.dtype), [], HOLD, (x, after))


def gather(x):
    below, above = along_z(x, 3), along_z(x, -3)
    three, two, three_later, two_later = kernel(
        pack_kernel, "pack", (blocks(3), blocks(2), blocks(3), blocks(2)), [], PACK, (x, below, above)
    )
    near = jnp.concatenate([three, along_z(three, 1), along_z(two, -1)])
    near_later = jnp.concatenate([three_later, along_z(three_later, 1), along_z(two_later, -1)])
    return near, near_later, three


def shards(fwd_queries, fwd_keyvals, bwd_queries, bwd_keyvals, bwd_cotangent, doc_lengths, block_order):
    lists = (jnp.concatenate([block_order, doc_lengths], axis=1),)
    near, near_later, three = gather(jnp.stack([bwd_keyvals, fwd_keyvals]))
    q_t, c_t, q_rows, c_rows, held = kernel(
        turn_kernel, "turn", (FLATS, FLATS, TALLS, TALLS, FLAT1), [], TURN,
        (bwd_queries, bwd_cotangent, across_x(bwd_queries), across_x(bwd_cotangent), fwd_queries, three),
    )
    mine = kernel(
        backward_stats_kernel, "backward_stats", STATS,
        [SCORES, SUMS, SUMS, SUMS], 2, (q_t, c_t, near), lists,
    )
    other = across_x(mine)
    dq, dq_far, keep, low, high = kernel(
        backward_kernel, "backward_grads", (FLAT1, FLAT1, blocks(3), blocks(3), blocks(2)),
        [SUMS, ACC, DKV, TURNED, PROBS, PROBS], GRADS, (q_t, c_t, q_rows, c_rows, near, mine, other), lists,
    )
    low, high = along_z(low, -1), along_z(high, 1)
    held = hold(held, mine)
    out, out_far = kernel(
        forward_kernel, "forward", (TALLER, TALLER),
        [FLAT, SCORES, SUMS, SUMS, ACC, TURNED, PROBS], FORWARD, (held, across_x(held), near_later, dq, dq_far), lists,
    )
    own, below, above = kernel(
        add_kernel, "add", (PART, PART, PART), [], ADD, (keep, low, high, out),
    )
    out, out_far = other_section(out), other_section(out_far, RING)
    own, below, above = other_section(own), other_section(below, 0, -3), other_section(above, 0, 3)
    query_grad, output, token = kernel(
        finish_kernel, "finish", (WHOLE, WHOLE, TOKEN), [], FINISH, (out, out_far)
    )
    keyval_grad = kernel(
        total_kernel, "total", blocks(1), [], 0, (own, below, above, token)
    )
    return output, query_grad, keyval_grad


def solution(mesh):
    placed = (
        P("pipe", "ctx", "tp"),
        P("pipe", None, "ctx", "tp"),
        P("pipe", "ctx", "tp"),
        P("pipe", None, "ctx", "tp"),
        P("pipe", "ctx", "tp"),
        P(),
        P(),
    )
    return jax.shard_map(
        shards,
        mesh=mesh,
        in_specs=placed,
        out_specs=(P("pipe", "ctx", "tp"), P("pipe", "ctx", "tp"), P("pipe", None, "ctx", "tp")),
        check_vma=False,
    )
```

```python
import jax
import jax.numpy as jnp
from jax import lax
from jax.experimental import pallas as pl
from jax.experimental.pallas import tpu as pltpu
from jax.sharding import PartitionSpec as P

HD = 128
BLOCK = 128
GROUP = 8
ROWS = GROUP * BLOCK
WIDE = 2 * BLOCK
SLOTS = 16
PAIRS = 2 * 8 + 2
BEYOND = 1 << 20
EXTRA = 8
FINAL = 2 * 128
PACK = 12
HOLD = 0
ADD = 12
GRADS = 40
TURN = 12
FORWARD = 12
FINISH = 4
RING = 8
OFFSETS = (0, -3, 3, -1, -4, 2, 1, -2)
SCALE = HD**-0.5
LOG2E = 1.4426950408889634
NEG = -1e30


def prepare(batch, table, slots, sides, bases, first, place):
    me = lax.axis_index("ctx")
    half, z = me // RING, me % RING
    query_bases, leasts = [], []
    for side in range(2):
        owner = (half + side) % 2 * RING + z
        query_base = table[batch, owner] * BLOCK
        at = query_base + lax.broadcasted_iota(jnp.int32, (8, BLOCK), 1)
        start = jnp.zeros((8, BLOCK), jnp.int32)
        least = jnp.int32(0)
        end = jnp.int32(0)
        for i in range(SLOTS, table.shape[1]):
            end = end + table[batch, i]
            start = jnp.where(at >= end, end, start)
            least = jnp.where(query_base >= end, end, least)
        first[side] = start
        place[side] = at
        query_bases.append(query_base)
        leasts.append(least)
    count = jnp.int32(0)
    for side in range(2):
        for slot in range(RING):
            owner = half * RING + (z + (OFFSETS[slot] + RING)) % RING
            base = table[batch, owner] * BLOCK
            slots[count] = slot
            sides[count] = side
            bases[count] = base
            active = (base <= query_bases[side]) & (base + (BLOCK - 1) >= leasts[side])
            count = count + active.astype(jnp.int32)
        slots[count] = 0
        bases[count] = BEYOND
        count = count + count % 2
    return count // 2


def dot(a, b):
    return jnp.dot(a, b, preferred_element_type=jnp.float32)


def add(*terms):
    total = terms[0].astype(jnp.float32)
    for term in terms[1:]:
        total = total + term.astype(jnp.float32)
    return total.astype(jnp.bfloat16)


def turn(ref, flat, tall=None):
    for h in range(GROUP):
        part = ref[0, :, h * HD : (h + 1) * HD]
        flat[:, h * BLOCK : (h + 1) * BLOCK] = part.T
        if tall is not None:
            tall[h * BLOCK : (h + 1) * BLOCK, :] = part


def total_kernel(own, below, above, _, out):
    out[0] = add(own[...], below[...], above[...])


def turn_kernel(q, c, q_far, c_far, later, _, q_t, c_t, q_rows, c_rows, held):
    turn(later, held.at[0])
    turn(q, q_t.at[0], q_rows.at[0])
    turn(c, c_t.at[0], c_rows.at[0])
    turn(q_far, q_t.at[1], q_rows.at[1])
    turn(c_far, c_t.at[1], c_rows.at[1])


def allowed(i, side, bases, first, place):
    row = bases[i] + lax.broadcasted_iota(jnp.int32, (BLOCK, BLOCK), 0)
    return (row >= first[side, 0:1]) & (row <= place[side, 0:1])


def masked_scores(key, q_t, side, mask, c):
    s = dot(key, q_t[side, :, c * WIDE : (c + 1) * WIDE])
    return [
        jnp.where(mask, s[:, j * BLOCK : (j + 1) * BLOCK], NEG) for j in range(WIDE // BLOCK)
    ]


def fold(x, op):
    return op(x.reshape(x.shape[0] // 8, 8, x.shape[1]), axis=0)


def largest(count, slots, sides, bases, first, place, kv, q_t, scores, tops):
    def body(g, _):
        side = sides[2 * g]
        keys = [kv[slots[2 * g + j], 0] for j in range(2)]
        masks = [allowed(2 * g + j, side, bases, first, place) for j in range(2)]
        for c in range(ROWS // WIDE):
            for j in range(2):
                for k, part in enumerate(masked_scores(keys[j], q_t, side, masks[j], c)):
                    at = slice(c * WIDE + k * BLOCK, c * WIDE + (k + 1) * BLOCK)
                    scores[2 * g + j, :, at] = part
                    tops[side, :, at] = jnp.maximum(tops[side, :, at], fold(part, jnp.max))
        return 0

    lax.fori_loop(0, count, body, 0)
    for side in range(2):
        tops[side] = jnp.broadcast_to(jnp.max(tops[side], axis=0, keepdims=True), (8, ROWS))


def statistics(count, slots, sides, bases, first, place, kv, q_t, c_t, scores, tops, totals, deltas):
    tops[...] = jnp.full(tops.shape, NEG, jnp.float32)
    totals[...] = jnp.zeros(totals.shape, jnp.float32)
    deltas[...] = jnp.zeros(deltas.shape, jnp.float32)

    largest(count, slots, sides, bases, first, place, kv, q_t, scores, tops)

    def sums(g, _):
        side = sides[2 * g]
        values = [kv[slots[2 * g + j], 1] for j in range(2)]
        for c in range(ROWS // WIDE):
            at = slice(c * WIDE, (c + 1) * WIDE)
            for j in range(2):
                p = jnp.exp2((scores[2 * g + j, :, at] - tops[side, 0:1, at]) * (SCALE * LOG2E))
                totals[side, :, at] += fold(p, jnp.sum)
                deltas[side, :, at] += fold(p * dot(values[j], c_t[side, :, at]), jnp.sum)
        return 0

    lax.fori_loop(0, count, sums, 0)
    rows = []
    for side in range(2):
        rows.append(tops[side, 0:1])
        rows.append(jnp.sum(totals[side], axis=0, keepdims=True))
        rows.append(jnp.sum(deltas[side], axis=0, keepdims=True))
    rows.append(jnp.zeros((8 - len(rows), ROWS), jnp.float32))
    return jnp.concatenate(rows, axis=0)


def merge(mine, other, per_side=3):
    merged = []
    for side in range(2):
        a = [mine[side * per_side + r : side * per_side + r + 1, :] for r in range(per_side)]
        b = [other[(1 - side) * per_side + r : (1 - side) * per_side + r + 1, :] for r in range(per_side)]
        top = jnp.maximum(a[0], b[0])
        fa = jnp.exp2((a[0] - top) * (SCALE * LOG2E))
        fb = jnp.exp2((b[0] - top) * (SCALE * LOG2E))
        merged.append([top] + [x * fa + y * fb for x, y in zip(a[1:], b[1:])])
    return merged


def backward_stats_kernel(
    table, q_t, c_t, near, out,
    slots, sides, bases, first, place, scores, tops, totals, deltas,
):
    count = prepare(0, table, slots, sides, bases, first, place)
    out[...] = statistics(
        count, slots, sides, bases, first, place, near, q_t, c_t, scores, tops, totals, deltas
    )


def thirds(x):
    parts = []
    for _ in range(3):
        part = x.astype(jnp.bfloat16).astype(jnp.float32)
        parts.append(part)
        x = x - part
    return parts


def forward_kernel(
    table, q, q_far, near, dq, dq_far, out, out_far,
    slots, sides, bases, first, place, q_t, scores, tops, totals, acc, turned, probs,
):
    count = prepare(1, table, slots, sides, bases, first, place)
    q_t[0], q_t[1] = q[0], q_far[0]
    tops[...] = jnp.full(tops.shape, NEG, jnp.float32)
    totals[...] = jnp.zeros(totals.shape, jnp.float32)
    acc[...] = jnp.zeros_like(acc)
    largest(count, slots, sides, bases, first, place, near, q_t, scores, tops)

    def body(g, _):
        side = sides[2 * g]
        for j in range(2):
            turned[:, j * BLOCK : (j + 1) * BLOCK] = near[slots[2 * g + j], 1].T
        for c in range(ROWS // WIDE):
            at = slice(c * WIDE, (c + 1) * WIDE)
            for j in range(2):
                p = jnp.exp2((scores[2 * g + j, :, at] - tops[side, 0:1, at]) * (SCALE * LOG2E))
                totals[side, :, at] += fold(p, jnp.sum)
                probs[j * BLOCK : (j + 1) * BLOCK, at] = p.astype(jnp.bfloat16)
        acc[side] += dot(turned[...], probs[...])
        return 0

    lax.fori_loop(0, count, body, 0)
    for side, (ref, grad) in enumerate(((out, dq), (out_far, dq_far))):
        ref[0, HD:FINAL] = grad[0]
        total = jnp.sum(totals[side], axis=0, keepdims=True)
        total = jnp.maximum(total, 1e-30)
        ref[0, :HD] = (acc[side] * (1.0 / total)).astype(jnp.bfloat16)
        logs = tops[side, 0:1] * (SCALE * LOG2E) + jnp.log2(total)
        pad = jnp.zeros((EXTRA - 3, ROWS), jnp.float32)
        ref[0, FINAL:] = jnp.concatenate(thirds(logs) + [pad], axis=0).astype(jnp.bfloat16)


def add_kernel(keep, low, high, _, own, below, above):
    own[...] = add(keep[0], low[0], high[0])
    below[...] = add(keep[1], low[1], high[1])
    above[...] = add(keep[2], low[2])


def pack_kernel(x, below, above, three, two, three_later, two_later):
    for batch, (wide, narrow) in enumerate(((three, two), (three_later, two_later))):
        for i, ref in enumerate((x, below, above)):
            wide[i] = ref[batch, 0]
            if i < 2:
                narrow[i] = ref[batch, 0]


def hold_kernel(x, _, out):
    out[...] = x[...]


def finish_kernel(a, b, query_grad, output, token):
    token[...] = jnp.zeros(token.shape, token.dtype)
    logs = []
    for ref in (a, b):
        rows = ref[0, FINAL:].astype(jnp.float32)
        logs.append(rows[0:1] + rows[1:2] + rows[2:3])
    top = jnp.maximum(logs[0], logs[1])
    wa, wb = jnp.exp2(logs[0] - top), jnp.exp2(logs[1] - top)
    inverse = 1.0 / (wa + wb)
    wa, wb = wa * inverse, wb * inverse
    for h in range(GROUP):
        at = slice(h * BLOCK, (h + 1) * BLOCK)
        x, y = a[0, :HD, at].astype(jnp.float32), b[0, :HD, at].astype(jnp.float32)
        output[0, :, at] = (x * wa[:, at] + y * wb[:, at]).astype(jnp.bfloat16).T
        query_grad[0, :, at] = add(a[0, HD:FINAL, at], b[0, HD:FINAL, at]).T


def backward_kernel(
    table, q_t, c_t, q_rows, c_rows, near, mine, other, dq, dq_far, keep, low, high,
    slots, sides, bases, first, place, rows, acc, dkv, turned, probs, dscores,
):
    count = prepare(0, table, slots, sides, bases, first, place)
    for side, (top, total, weighted) in enumerate(merge(mine, other)):
        rows[side, 0:1] = top * (SCALE * LOG2E) + jnp.log2(total)
        rows[side, 1:2] = weighted / total
    acc[...] = jnp.zeros_like(acc)
    dkv[...] = jnp.zeros_like(dkv)

    def grads(g, _):
        side = sides[2 * g]
        for j in range(2):
            at_rows = slice(j * BLOCK, (j + 1) * BLOCK)
            key = near[slots[2 * g + j], 0]
            value = near[slots[2 * g + j], 1]
            mask = allowed(2 * g + j, side, bases, first, place)
            turned[:, at_rows] = key.T
            for c in range(ROWS // WIDE):
                at = slice(c * WIDE, (c + 1) * WIDE)
                s = jnp.concatenate(masked_scores(key, q_t, side, mask, c), axis=1)
                p = jnp.exp2(s * (SCALE * LOG2E) - rows[side, 0:1, at])
                dp = dot(value, c_t[side, :, at])
                probs[at_rows, at] = p.astype(jnp.bfloat16)
                dscores[at_rows, at] = (p * (dp - rows[side, 1:2, at])).astype(jnp.bfloat16)
        dv = dot(probs[...], c_rows[side])
        dk = dot(dscores[...], q_rows[side]) * SCALE
        acc[side] += dot(turned[...], dscores[...])
        for j in range(2):
            at_rows = slice(j * BLOCK, (j + 1) * BLOCK)
            dkv[slots[2 * g + j], 0] += dk[at_rows]
            dkv[slots[2 * g + j], 1] += dv[at_rows]
        return 0

    lax.fori_loop(0, count, grads, 0)
    keep[...] = dkv[0:3].astype(jnp.bfloat16)
    low[...] = dkv[3:6].astype(jnp.bfloat16)
    high[...] = dkv[6:8].astype(jnp.bfloat16)
    for side, ref in enumerate((dq, dq_far)):
        ref[0] = (acc[side] * SCALE).astype(jnp.bfloat16)


SMEM = pl.BlockSpec(memory_space=pltpu.SMEM)
VMEM = pl.BlockSpec(memory_space=pltpu.VMEM)
WHOLE = jax.ShapeDtypeStruct((1, BLOCK, GROUP * HD), jnp.bfloat16)
TOKEN = jax.ShapeDtypeStruct((8, 128), jnp.float32)
STATS = jax.ShapeDtypeStruct((8, ROWS), jnp.float32)
LIST = pltpu.SMEM((PAIRS + 1,), jnp.int32)
PLACES = pltpu.VMEM((2, 8, BLOCK), jnp.int32)
LISTS = [LIST, LIST, LIST, PLACES, PLACES]
TALLS = jax.ShapeDtypeStruct((2, ROWS, HD), jnp.bfloat16)
FLAT1 = jax.ShapeDtypeStruct((1, HD, ROWS), jnp.bfloat16)
FLATS = jax.ShapeDtypeStruct((2, HD, ROWS), jnp.bfloat16)
FLAT = pltpu.VMEM((2, HD, ROWS), jnp.bfloat16)
PART = jax.ShapeDtypeStruct((2, BLOCK, HD), jnp.bfloat16)
TALLER = jax.ShapeDtypeStruct((1, FINAL + EXTRA, GROUP * HD), jnp.bfloat16)
SCORES = pltpu.VMEM((PAIRS, BLOCK, ROWS), jnp.float32)
ACC = pltpu.VMEM((2, HD, ROWS), jnp.float32)
TURNED = pltpu.VMEM((HD, 2 * BLOCK), jnp.bfloat16)
PROBS = pltpu.VMEM((2 * BLOCK, ROWS), jnp.bfloat16)
SUMS = pltpu.VMEM((2, 8, ROWS), jnp.float32)
DKV = pltpu.VMEM((RING, 2, BLOCK, HD), jnp.float32)


def blocks(n):
    return jax.ShapeDtypeStruct((n, 2, BLOCK, HD), jnp.bfloat16)


def kernel(body, name, outs, scratch, cost, args, lists=()):
    single = not isinstance(outs, tuple)
    return pl.pallas_call(
        body,
        out_shape=outs,
        in_specs=[SMEM] * len(lists) + [VMEM] * len(args),
        out_specs=VMEM if single else (VMEM,) * len(outs),
        scratch_shapes=(LISTS if lists else []) + scratch,
        compiler_params=pltpu.CompilerParams(vmem_limit_bytes=32 << 20),
        cost_estimate=pl.CostEstimate(
            flops=cost << 29, bytes_accessed=2 << 20, transcendentals=1 << 21
        ),
        name=name,
    )(*lists, *args)


def along_z(x, distance):
    route = [(i, i // RING * RING + (i + distance) % RING) for i in range(SLOTS)]
    return lax.ppermute(x, "ctx", route)


def across_x(x):
    return lax.ppermute(x, "ctx", [(i, i ^ RING) for i in range(SLOTS)])


def other_section(x, flip=0, distance=0):
    route = [
        (p * SLOTS + i, (1 - p) * SLOTS + (i // RING * RING + (i + distance) % RING ^ flip))
        for p in range(2)
        for i in range(SLOTS)
    ]
    return lax.ppermute(x, ("pipe", "ctx"), route)


def hold(x, after):
    return kernel(hold_kernel, "hold", jax.ShapeDtypeStruct(x.shape, x.dtype), [], HOLD, (x, after))


def gather(x):
    below, above = along_z(x, 3), along_z(x, -3)
    three, two, three_later, two_later = kernel(
        pack_kernel, "pack", (blocks(3), blocks(2), blocks(3), blocks(2)), [], PACK, (x, below, above)
    )
    near = jnp.concatenate([three, along_z(three, 1), along_z(two, -1)])
    near_later = jnp.concatenate([three_later, along_z(three_later, 1), along_z(two_later, -1)])
    return near, near_later, three


def shards(fwd_queries, fwd_keyvals, bwd_queries, bwd_keyvals, bwd_cotangent, doc_lengths, block_order):
    lists = (jnp.concatenate([block_order, doc_lengths], axis=1),)
    near, near_later, three = gather(jnp.stack([bwd_keyvals, fwd_keyvals]))
    q_t, c_t, q_rows, c_rows, held = kernel(
        turn_kernel, "turn", (FLATS, FLATS, TALLS, TALLS, FLAT1), [], TURN,
        (bwd_queries, bwd_cotangent, across_x(bwd_queries), across_x(bwd_cotangent), fwd_queries, three),
    )
    mine = kernel(
        backward_stats_kernel, "backward_stats", STATS,
        [SCORES, SUMS, SUMS, SUMS], 2, (q_t, c_t, near), lists,
    )
    other = across_x(mine)
    dq, dq_far, keep, low, high = kernel(
        backward_kernel, "backward_grads", (FLAT1, FLAT1, blocks(3), blocks(3), blocks(2)),
        [SUMS, ACC, DKV, TURNED, PROBS, PROBS], GRADS, (q_t, c_t, q_rows, c_rows, near, mine, other), lists,
    )
    low, high = along_z(low, -1), along_z(high, 1)
    held = hold(held, mine)
    out, out_far = kernel(
        forward_kernel, "forward", (TALLER, TALLER),
        [FLAT, SCORES, SUMS, SUMS, ACC, TURNED, PROBS], FORWARD, (held, across_x(held), near_later, dq, dq_far), lists,
    )
    own, below, above = kernel(
        add_kernel, "add", (PART, PART, PART), [], ADD, (keep, low, high, out),
    )
    out, out_far = other_section(out), other_section(out_far, RING)
    below, above = other_section(below, 0, -3), other_section(above, 0, 3)
    own = other_section(own)
    query_grad, output, token = kernel(
        finish_kernel, "finish", (WHOLE, WHOLE, TOKEN), [], FINISH, (out, out_far)
    )
    keyval_grad = kernel(
        total_kernel, "total", blocks(1), [], 0, (own, below, above, token)
    )
    return output, query_grad, keyval_grad


def solution(mesh):
    placed = (
        P("pipe", "ctx", "tp"),
        P("pipe", None, "ctx", "tp"),
        P("pipe", "ctx", "tp"),
        P("pipe", None, "ctx", "tp"),
        P("pipe", "ctx", "tp"),
        P(),
        P(),
    )
    return jax.shard_map(
        shards,
        mesh=mesh,
        in_specs=placed,
        out_specs=(P("pipe", "ctx", "tp"), P("pipe", "ctx", "tp"), P("pipe", None, "ctx", "tp")),
        check_vma=False,
    )
```
